32 devices in a mesh: groups: 2 (over y), tensor: 4 (over z), replica: 4 (over x, core).
Axes of the slice: x: 2, y: 2, z: 4, core: 2. Of those that a mesh axis runs over, the one named last changes fastest.
Arguments:
- hidden: bfloat16 [32, 2, 8192], P(('groups', 'replica')), parts along dimension 0, may hold values from -32 to 32
- query: bfloat16 [32, 2, 512], P(('groups', 'replica'), None, 'tensor'), parts along dimension 0, may hold values from -96 to 96
- incoming_key_value: bfloat16 [32, 2, 4, 256], P(('groups', 'replica'), None, 'tensor'), parts along dimension 0, may hold values from -4 to 4, as said below
- cache: bfloat16 [32, 256, 4, 256], P(('groups', 'replica'), None, 'tensor'), parts along dimension 0, may hold values from -4 to 4, as said below
- lengths: int32 [32], P(('groups', 'replica')), parts along dimension 0, may hold values from 2 to 256, as said below
- output_projection_weight: bfloat16 [512, 8192], P('tensor'), may hold values from -0.25 to 0.25
- adapter_down_factor: bfloat16 [128, 512], P(('groups', 'tensor')), parts along dimension 0, may hold values from -0.25 to 0.25
- adapter_up_factor: bfloat16 [16384, 64], P(('groups', 'tensor', 'replica')), parts along dimension 0, may hold values from -0.75 to 0.75
- gain: float32 [8192], replicated, may hold values from 0.1 to 1.9
Outputs:
- normed: bfloat16 [32, 2, 8192], P(('groups', 'replica')), parts along dimension 0
- merged: bfloat16 [1024, 8192], P(('groups', 'tensor')), parts along dimension 0
The draws below stay inside these ranges and needn't reach their ends.
There are 2 independent parts, one for each index of `groups`. The reference program is written for one: setup_inputs(seed, part) draws one part's arguments, and reference() takes and returns one part's arrays. A program takes and returns all parts, laid end to end along the dimension named above; an argument that names none is the same for every part. Nothing has to cross between parts.
Inputs may be any that keep to these rules, and one draw needn't show every extreme that they name: `cache`: the slots of the 1 consecutive query heads of one group are equal. `incoming_key_value`: the slots of the 1 consecutive query heads of one group are equal. `lengths`: some row has exactly 256.
All inputs are finite; a program needn't handle non-finite values.
Results may differ from the reference program's by a relative error of at most 0.0052.
Values may be sent and summed in bfloat16 or wider, within the bound.
A program may use at most 64 MiB of HBM per device.

```python
import math
import jax
import jax.numpy as jnp
from jax import lax

MODEL_WIDTH = 8192
HEAD_SIZE = 128
ADAPTER_RANK = 64
NEW = 2
CACHE = 256
QUERY_HEADS = 4
KV_HEADS = 4
ROWS = 16


def spread_heads(values, head_axis):
    return jnp.repeat(values, QUERY_HEADS // KV_HEADS, axis=head_axis)


def first_keys(key):
    drawn = jax.random.truncated_normal(jax.random.fold_in(key, 101), -4.0, 4.0, (ROWS, KV_HEADS, HEAD_SIZE), jnp.float32)
    return spread_heads(drawn, 1)


def draw_hidden(key, part):
    key = jax.random.fold_in(key, 3)
    key_one, key_two = jax.random.split(key, 2)
    normal_part = jax.random.truncated_normal(key_one, -4.0, 4.0, (ROWS, NEW, MODEL_WIDTH), jnp.float32)
    position = jnp.arange(MODEL_WIDTH, dtype=jnp.float32) / MODEL_WIDTH
    rough = jnp.exp(jax.random.uniform(key_two, (MODEL_WIDTH,), jnp.float32, -1.15, 1.15))
    values = 0.15 * normal_part * 3.0 ** position * rough
    return jnp.clip(values, -32.0, 32.0).astype(jnp.bfloat16)


def draw_query(key, part):
    key = jax.random.fold_in(key, 9)
    key_one = jax.random.fold_in(key, 0)
    queries = jax.random.truncated_normal(key_one, -4.0, 4.0, (ROWS, NEW, QUERY_HEADS, HEAD_SIZE), jnp.float32)
    return queries.reshape(ROWS, NEW, QUERY_HEADS * HEAD_SIZE).astype(jnp.bfloat16)


def draw_incoming_key_value(key, part):
    key = jax.random.fold_in(key, 11)
    values = jax.random.truncated_normal(key, -4.0, 4.0, (ROWS, NEW, KV_HEADS, 2 * HEAD_SIZE), jnp.float32)
    return spread_heads(values, 2).astype(jnp.bfloat16)


def draw_cache(key, part):
    leading = first_keys(key)
    key = jax.random.fold_in(key, 5)
    values = jax.random.truncated_normal(key, -4.0, 4.0, (ROWS, CACHE, KV_HEADS, 2 * HEAD_SIZE), jnp.float32)
    values = spread_heads(values, 2)
    padded = jnp.concatenate([leading, jnp.zeros((ROWS, QUERY_HEADS, HEAD_SIZE), jnp.float32)], axis=2)[:, None, :, :]
    position = jnp.arange(CACHE, dtype=jnp.int32)[None, :, None, None]
    is_key = jnp.arange(2 * HEAD_SIZE, dtype=jnp.int32)[None, None, None, :] < HEAD_SIZE
    values = jnp.where((position == 0) & is_key, padded, values)
    return values.astype(jnp.bfloat16)


def draw_lengths(key, part):
    key = jax.random.fold_in(key, 7)
    key_one, key_two = jax.random.split(key)
    spans = jax.random.randint(key_one, (ROWS,), 2, CACHE + 1, jnp.int32)
    longest = jax.random.randint(key_two, (), 0, ROWS, jnp.int32)
    return jnp.where(jnp.arange(ROWS, dtype=jnp.int32) == longest, CACHE, spans).astype(jnp.int32)


def levels(own_key, shape, pieces, low, largest):
    loudness, own = 1.0, jax.random.fold_in(own_key, 6)
    for axis_at, parts in pieces:
        steps = jnp.exp(jax.random.uniform(jax.random.fold_in(own, axis_at), (parts,), jnp.float32, low / len(pieces), largest / len(pieces)))
        loudness = loudness * jnp.repeat(steps, shape[axis_at] // parts).reshape([-1 if axis == axis_at else 1 for axis in range(len(shape))])
    return loudness


def normal_values(own_key, extent, spread, bound, shards=(), kind=jnp.bfloat16):
    values = spread * jax.random.normal(own_key, extent, jnp.float32)
    if shards:
        values = values * levels(own_key, extent, shards, -0.22, 0.18)
    return jnp.clip(values, -bound, bound).astype(kind)


def setup_inputs(seed: int = 0, part: int = 0) -> dict:
    key_of = jax.random.split(jax.random.key(seed), 10)
    part_keys = jax.random.split(jax.random.fold_in(key_of[9], part), 10)
    hidden = draw_hidden(jax.random.fold_in(jax.random.fold_in(key_of[9], part), 71), part)
    query = draw_query(jax.random.fold_in(jax.random.fold_in(key_of[9], part), 71), part)
    incoming_key_value = draw_incoming_key_value(jax.random.fold_in(jax.random.fold_in(key_of[9], part), 71), part)
    cache = draw_cache(jax.random.fold_in(jax.random.fold_in(key_of[9], part), 71), part)
    lengths = draw_lengths(jax.random.fold_in(jax.random.fold_in(key_of[9], part), 71), part)
    output_projection_weight = normal_values(key_of[5], (QUERY_HEADS * HEAD_SIZE, MODEL_WIDTH), (QUERY_HEADS * HEAD_SIZE) ** -0.5, 0.25, ((0, 4),))
    adapter_down_factor = normal_values(part_keys[6], (ADAPTER_RANK, QUERY_HEADS * HEAD_SIZE), (QUERY_HEADS * HEAD_SIZE) ** -0.5, 0.25, ((0, 4),))
    adapter_up_factor = normal_values(part_keys[7], (MODEL_WIDTH, ADAPTER_RANK), ADAPTER_RANK ** -0.5, 0.75, ((0, 16),))
    gain = jnp.clip(1.0 + 0.18 * jax.random.normal(key_of[8], (MODEL_WIDTH,), jnp.float32), 0.1, 1.9)
    return dict(hidden=hidden, query=query, incoming_key_value=incoming_key_value, cache=cache, lengths=lengths, output_projection_weight=output_projection_weight, adapter_down_factor=adapter_down_factor, adapter_up_factor=adapter_up_factor, gain=gain)


ADAPTER_SCALE = 2.0
EPS = 1e-06

def attend(query, incoming_key_value, cache, lengths):
    row_count = query.shape[0]
    queries = query.reshape(row_count, NEW, QUERY_HEADS, HEAD_SIZE).astype(jnp.float32)
    scale_factor = 1.0 / math.sqrt(HEAD_SIZE)
    keys = cache[..., :HEAD_SIZE].astype(jnp.float32)
    values = cache[..., HEAD_SIZE:].astype(jnp.float32)
    fresh_keys = incoming_key_value[..., :HEAD_SIZE].astype(jnp.float32)
    fresh_values = incoming_key_value[..., HEAD_SIZE:].astype(jnp.float32)
    older = jnp.einsum('rihd,rlhd->rihl', queries, keys) * scale_factor
    fresh = jnp.einsum('rihd,rjhd->rihj', queries, fresh_keys) * scale_factor
    live_old = jnp.arange(CACHE, dtype=jnp.int32)[None, None, None, :] < lengths[:, None, None, None]
    live_new = jnp.arange(NEW, dtype=jnp.int32)[None, None, None, :] <= jnp.arange(NEW, dtype=jnp.int32)[None, :, None, None]
    scores = jnp.concatenate([jnp.where(live_old, older, -1e+30), jnp.where(live_new, fresh, -1e+30)], axis=3)
    weights = jax.nn.softmax(scores, axis=3).astype(jnp.bfloat16).astype(jnp.float32)
    mixed = jnp.einsum('rihl,rlhd->rihd', weights[..., :CACHE], values)
    mixed = mixed + jnp.einsum('rihj,rjhd->rihd', weights[..., CACHE:], fresh_values)
    return mixed.astype(jnp.bfloat16).reshape(row_count, NEW, QUERY_HEADS * HEAD_SIZE)

def reference(hidden, query, incoming_key_value, cache, lengths, output_projection_weight, adapter_down_factor, adapter_up_factor, gain):
    context = attend(query, incoming_key_value, cache, lengths)
    adapter_update = jnp.dot(adapter_down_factor.T, adapter_up_factor.T, preferred_element_type=jnp.float32)
    merged = (output_projection_weight.astype(jnp.float32) + ADAPTER_SCALE * adapter_update).astype(jnp.bfloat16)
    attention = jnp.dot(context.reshape(ROWS * NEW, QUERY_HEADS * HEAD_SIZE), merged, preferred_element_type=jnp.float32)
    resid = hidden.astype(jnp.float32) + attention.reshape(ROWS, NEW, MODEL_WIDTH)
    mean_square = lax.optimization_barrier(jnp.mean(resid * resid, axis=-1, keepdims=True))
    normed = (resid * lax.rsqrt(mean_square + EPS) * gain).astype(jnp.bfloat16)
    return (normed, merged)
```

```python
import functools
import math

import jax
import jax.numpy as jnp
from jax import lax
from jax.experimental import pallas as pl
from jax.experimental.pallas import tpu as pltpu
from jax.sharding import PartitionSpec as P

HEAD_SIZE = 128


ADAPTER_SCALE = 2.0
EPS = 1e-06


def attend(query, incoming_key_value, cache, lengths):
    row_count, steps, features = query.shape
    heads = features // HEAD_SIZE
    span = cache.shape[1]
    queries = query.reshape(row_count, steps, heads, HEAD_SIZE)
    scale_factor = 1.0 / math.sqrt(HEAD_SIZE)
    older = (
        jnp.einsum(
            "rihd,rlhd->rihl", queries, cache[..., :HEAD_SIZE], preferred_element_type=jnp.float32
        )
        * scale_factor
    )
    fresh = (
        jnp.einsum(
            "rihd,rjhd->rihj",
            queries,
            incoming_key_value[..., :HEAD_SIZE],
            preferred_element_type=jnp.float32,
        )
        * scale_factor
    )
    live_old = jnp.arange(span, dtype=jnp.int32)[None, None, None, :] < lengths[:, None, None, None]
    live_new = (
        jnp.arange(steps, dtype=jnp.int32)[None, None, None, :]
        <= jnp.arange(steps, dtype=jnp.int32)[None, :, None, None]
    )
    scores = jnp.concatenate(
        [jnp.where(live_old, older, -1e30), jnp.where(live_new, fresh, -1e30)], axis=3
    )
    weights = jax.nn.softmax(scores, axis=3).astype(jnp.bfloat16)
    mixed = jnp.einsum(
        "rihl,rlhd->rihd",
        weights[..., :span],
        cache[..., HEAD_SIZE:],
        preferred_element_type=jnp.float32,
    )
    mixed = mixed + jnp.einsum(
        "rihj,rjhd->rihd",
        weights[..., span:],
        incoming_key_value[..., HEAD_SIZE:],
        preferred_element_type=jnp.float32,
    )
    return mixed.astype(jnp.bfloat16).reshape(row_count, steps, features)


def per_device(
    hidden,
    query,
    incoming_key_value,
    cache,
    lengths,
    output_projection_weight,
    adapter_down_factor,
    adapter_up_factor,
    gain,
):
    context = attend(query, incoming_key_value, cache, lengths)
    owned = output_projection_weight.shape[0]
    complete_down_factor = lax.all_gather(adapter_down_factor, "tensor", axis=0, tiled=True)
    a_columns = lax.dynamic_slice_in_dim(
        complete_down_factor, lax.axis_index("tensor") * owned, owned, 1
    )
    adapter_update = lax.dot_general(
        a_columns,
        lax.all_gather(adapter_up_factor, ("tensor", "replica"), axis=0, tiled=True),
        (((0,), (1,)), ((), ())),
        preferred_element_type=jnp.float32,
    )
    merged = (output_projection_weight.astype(jnp.float32) + ADAPTER_SCALE * adapter_update).astype(
        jnp.bfloat16
    )
    row_count, steps = (context.shape[0], context.shape[1])
    partial_value = jnp.dot(
        context.reshape(row_count * steps, owned), merged, preferred_element_type=jnp.float32
    )
    partial_value = partial_value.reshape(row_count, steps, merged.shape[1])
    summed = lax.psum(partial_value, "tensor")
    resid = hidden.astype(jnp.float32) + summed
    mean_square = jnp.mean(resid * resid, axis=-1, keepdims=True)
    normed = (resid * lax.rsqrt(mean_square + EPS) * gain).astype(jnp.bfloat16)
    return (normed, merged)


MESH = pl.DeviceIdType.MESH
F32 = jnp.float32
BF16 = jnp.bfloat16


def fused_kernel(
    sizes,
    lengths_ref,
    hidden_hbm,
    query_hbm,
    fresh_hbm,
    cache_hbm,
    weight_hbm,
    down_hbm,
    up_hbm,
    gain_hbm,
    normed_ref,
    merged_hbm,
    hidden_ref,
    query_ref,
    fresh_ref,
    cache_ref,
    weight_ref,
    gain_ref,
    down_all,
    up_all,
    queries,
    fresh_rows,
    hidden_rows,
    context_out,
    context_in,
    part_out,
    part_in,
    square_out,
    square_in,
    resid_out,
    resid_in,
    own_sum,
    own_resid,
    load_sem,
    store_sem,
    z_send,
    z_recv,
    x_send,
    x_recv,
    c_send,
    c_recv,
    a_send,
    a_recv,
    ctx_send,
    ctx_recv,
    rs_send,
    rs_recv,
    sq_send,
    sq_recv,
    ag_send,
    ag_recv,
):
    rows, steps, span, width, owned, n = sizes
    count = rows * steps
    part = width // n
    half = part // 2
    chunk = up_hbm.shape[1]
    rank_part = down_hbm.shape[0]
    t = lax.axis_index("tensor")
    r = lax.axis_index("replica")
    across = lax.rem(r + 2, 4)
    beside = r + 1 - 2 * lax.rem(r, 2)
    me = t * 4 + r

    def ahead(k):
        return lax.rem(t + k, n)

    def behind(k):
        return lax.rem(t + n - k, n)

    def remote(source, target, send, recv, device):
        return pltpu.make_async_remote_copy(
            src_ref=source,
            dst_ref=target,
            send_sem=send,
            recv_sem=recv,
            device_id=device,
            device_id_type=MESH,
        )

    mine = pl.ds(pl.multiple_of(t * rank_part, rank_part), rank_part)
    loads = [
        pltpu.make_async_copy(a, b, load_sem.at[i])
        for i, (a, b) in enumerate(
            [
                (up_hbm, up_all.at[me]),
                (down_hbm, down_all.at[mine]),
                (query_hbm, query_ref),
                (fresh_hbm, fresh_ref),
                (cache_hbm, cache_ref),
                (weight_hbm, weight_ref),
                (hidden_hbm, hidden_ref),
                (gain_hbm, gain_ref),
            ]
        )
    ]
    for load in loads:
        load.start()

    barrier = pltpu.get_barrier_semaphore()
    for k in range(1, n):
        pl.semaphore_signal(barrier, inc=1, device_id={"tensor": ahead(k)}, device_id_type=MESH)
    pl.semaphore_signal(barrier, inc=1, device_id={"replica": across}, device_id_type=MESH)
    pl.semaphore_signal(barrier, inc=1, device_id={"replica": beside}, device_id_type=MESH)

    z_copies = [
        remote(up_all.at[me], up_all.at[me], z_send.at[k - 1], z_recv.at[k - 1], {"tensor": ahead(k)})
        for k in range(1, n)
    ]
    x_copies = []
    c_copies = []
    for k in range(n):
        near = behind(k) * 4 + r
        far = behind(k) * 4 + across
        x_copies.append(
            remote(up_all.at[near], up_all.at[near], x_send.at[k], x_recv.at[k], {"replica": across})
        )
        for j, slot in enumerate((near, far)):
            i = 2 * k + j
            c_copies.append(
                remote(up_all.at[slot], up_all.at[slot], c_send.at[i], c_recv.at[i], {"replica": beside})
            )
    a_copies = [
        remote(
            down_all.at[mine], down_all.at[mine], a_send.at[k - 1], a_recv.at[k - 1], {"tensor": ahead(k)}
        )
        for k in range(1, n)
    ]

    loads[0].wait()
    loads[1].wait()
    pl.semaphore_wait(barrier, n + 1)
    x_copies[0].start()
    c_copies[0].start()
    for k in (2, 1, 3):
        z_copies[k - 1].start()
    for copy in a_copies:
        copy.start()

    loads[2].wait()
    loads[3].wait()
    for i in range(rows):
        queries[i * steps : (i + 1) * steps, :] = query_ref[i].astype(F32)
        fresh_rows[i * steps : (i + 1) * steps, :] = fresh_ref[i].astype(F32)
    q = queries[...].astype(BF16)
    fresh = fresh_rows[...].astype(BF16)
    scale_factor = 1.0 / math.sqrt(HEAD_SIZE)
    contract = (((1,), (1,)), ((), ()))
    loads[4].wait()
    keys = cache_ref[:, :, :HEAD_SIZE].reshape(rows * span, HEAD_SIZE)
    values = cache_ref[:, :, HEAD_SIZE:].reshape(rows * span, HEAD_SIZE)
    older = lax.dot_general(q, keys, contract, preferred_element_type=F32) * scale_factor
    newer = lax.dot_general(
        q, fresh[:, :HEAD_SIZE], contract, preferred_element_type=F32
    ) * scale_factor
    row = lax.broadcasted_iota(jnp.int32, (count, rows * span), 0)
    column = lax.broadcasted_iota(jnp.int32, (count, rows * span), 1)
    low = (row // steps) * span
    high = low
    for i in range(rows):
        high = jnp.where(row // steps == i, i * span + lengths_ref[i], high)
    older = jnp.where((column >= low) & (column < high), older, -1e30)
    row = lax.broadcasted_iota(jnp.int32, (count, count), 0)
    column = lax.broadcasted_iota(jnp.int32, (count, count), 1)
    keep = (row // steps == column // steps) & (column <= row)
    newer = jnp.where(keep, newer, -1e30)
    top = jnp.maximum(
        jnp.max(older, axis=1, keepdims=True), jnp.max(newer, axis=1, keepdims=True)
    )
    older = jnp.exp(older - top)
    newer = jnp.exp(newer - top)
    total = jnp.sum(older, axis=1, keepdims=True) + jnp.sum(newer, axis=1, keepdims=True)
    older = (older / total).astype(BF16)
    newer = (newer / total).astype(BF16)
    context = jnp.dot(older, values, preferred_element_type=F32)
    context = context + jnp.dot(newer, fresh[:, HEAD_SIZE:], preferred_element_type=F32)
    context16 = jnp.concatenate([context, jnp.zeros_like(context)], axis=0).astype(BF16)
    context_out[...] = context16
    ctx_copies = [
        remote(
            context_out,
            context_in.at[k - 1],
            ctx_send.at[k - 1],
            ctx_recv.at[k - 1],
            {"tensor": ahead(k)},
        )
        for k in range(1, n)
    ]
    for copy in ctx_copies:
        copy.start()

    def columns(owner):
        return pl.ds(pl.multiple_of(owner * part, part), part)

    context = context_out[...]
    loads[5].wait()
    rs_copies = [None] * n
    for k in (2, 1, 3):
        product = jnp.dot(context, weight_ref[:, columns(ahead(k))], preferred_element_type=F32)
        part_out[k - 1] = jnp.concatenate(
            [product[:count, :half], product[:count, half:]], axis=0
        ).astype(BF16)
        rs_copies[k] = remote(
            part_out.at[k - 1],
            part_in.at[k - 1],
            rs_send.at[k - 1],
            rs_recv.at[k - 1],
            {"tensor": ahead(k)},
        )
        rs_copies[k].start()
    x_copies[0].wait_recv()
    c_copies[1].start()
    for k in range(1, n):
        z_copies[k - 1].wait_recv()
        x_copies[k].start()
        c_copies[2 * k].start()
    loads[6].wait()
    for i in range(rows):
        hidden_rows[i * steps : (i + 1) * steps, :] = hidden_ref[i, :, columns(t)].astype(F32)
    product = jnp.dot(context, weight_ref[:, columns(t)], preferred_element_type=F32)
    own_sum[...] = product[:count] + hidden_rows[...]

    for copy in a_copies:
        copy.wait_recv()
    head = pl.ds(pl.multiple_of(t * owned, owned), owned)
    own_down = (down_all[:, head].astype(F32) * ADAPTER_SCALE).T.astype(BF16)
    stores = []

    def merge(slot):
        place = pl.ds(pl.multiple_of(slot * chunk, chunk), chunk)
        update = jnp.dot(own_down, up_all[slot], preferred_element_type=F32)
        weight_ref[:, place] = (weight_ref[:, place].astype(F32) + update).astype(BF16)
        copy = pltpu.make_async_copy(
            weight_ref.at[:, place], merged_hbm.at[:, place], store_sem.at[len(stores)]
        )
        copy.start()
        stores.append(copy)

    for k in range(n):
        merge(behind(k) * 4 + r)

    for copy in ctx_copies:
        copy.wait_recv()
    inner = jnp.dot(context, own_down, preferred_element_type=F32)
    for k in range(1, n):
        other = pl.ds(pl.multiple_of(behind(k) * owned, owned), owned)
        inner = inner + ADAPTER_SCALE * lax.dot_general(
            context_in[k - 1], down_all[:, other], contract, preferred_element_type=F32
        )
    inner = inner[:count]
    upper = inner.astype(BF16).astype(F32)
    inner = jnp.concatenate([upper, inner - upper], axis=0).astype(BF16)
    c_copies[0].wait_recv()
    c_copies[1].wait_recv()
    for k in range(1, n):
        rs_copies[k].wait_recv()
    squares = jnp.zeros((count, 1), F32)
    pieces = []
    for j in range(4):
        place = slice(j * chunk, (j + 1) * chunk)
        term = jnp.dot(inner, up_all[t * 4 + j], preferred_element_type=F32)
        value = own_sum[:, place] + term[:count] + term[count:]
        for k in range(1, n):
            top_rows = (j * chunk) // half * count
            start = (j * chunk) % half
            value = value + part_in[k - 1, :, start : start + chunk].astype(F32)[
                top_rows : top_rows + count
            ]
        squares = squares + jnp.sum(value * value, axis=1, keepdims=True)
        own_resid[:, place] = value
        pieces.append(value)
    square_out[...] = jnp.broadcast_to(squares, square_out.shape)
    resid_out[...] = jnp.concatenate(
        [
            jnp.concatenate([pieces[0], pieces[1]], axis=1),
            jnp.concatenate([pieces[2], pieces[3]], axis=1),
        ],
        axis=0,
    ).astype(BF16)
    ag_copies = []
    for k in (2, 1, 3):
        device = {"tensor": ahead(k)}
        copies = [
            remote(square_out, square_in.at[k - 1], sq_send.at[k - 1], sq_recv.at[k - 1], device),
            remote(resid_out, resid_in.at[k - 1], ag_send.at[k - 1], ag_recv.at[k - 1], device),
        ]
        for copy in copies:
            copy.start()
        ag_copies.append((k, copies))

    for k in range(1, n):
        x_copies[k].wait_recv()
        c_copies[2 * k + 1].start()
    for k in range(n):
        merge(behind(k) * 4 + across)
    opposite = lax.rem(beside + 2, 4)
    for k in range(n):
        if k:
            c_copies[2 * k].wait_recv()
        merge(behind(k) * 4 + beside)
    for k in range(n):
        if k:
            c_copies[2 * k + 1].wait_recv()
        merge(behind(k) * 4 + opposite)

    for k, copies in ag_copies:
        copies[0].wait_recv()
        squares = squares + square_in[k - 1, :, :1]
    factor = lax.rsqrt(squares / width + EPS)
    loads[7].wait()
    value = own_resid[...] * factor * gain_ref[:, columns(t)]
    for i in range(rows):
        normed_ref[i, :, columns(t)] = value[i * steps : (i + 1) * steps].astype(BF16)
    for k, copies in ag_copies:
        copies[1].wait_recv()
        arrived = resid_in[k - 1].astype(F32)
        value = jnp.concatenate([arrived[:count], arrived[count:]], axis=1)
        place = columns(behind(k))
        value = value * factor * gain_ref[:, place]
        for i in range(rows):
            normed_ref[i, :, place] = value[i * steps : (i + 1) * steps].astype(BF16)

    for copy in z_copies + x_copies + c_copies + a_copies + ctx_copies + rs_copies[1:]:
        copy.wait_send()
    for k, copies in ag_copies:
        for copy in copies:
            copy.wait_send()
    for copy in stores:
        copy.wait()


def fused(
    hidden,
    query,
    incoming_key_value,
    cache,
    lengths,
    output_projection_weight,
    adapter_down_factor,
    adapter_up_factor,
    gain,
):
    rows, steps, width = hidden.shape
    span = cache.shape[1]
    owned = output_projection_weight.shape[0]
    n = adapter_down_factor.shape[1] // owned
    rank = adapter_up_factor.shape[1]
    chunk = adapter_up_factor.shape[0]
    count = rows * steps
    part = width // n
    half = part // 2
    both = 2 * HEAD_SIZE
    anywhere = pl.BlockSpec(memory_space=pl.ANY)
    dma = pltpu.SemaphoreType.DMA
    peers = n - 1
    return pl.pallas_call(
        functools.partial(fused_kernel, (rows, steps, span, width, owned, n)),
        out_shape=(
            jax.ShapeDtypeStruct((rows, steps, width), BF16),
            jax.ShapeDtypeStruct((owned, width), BF16),
        ),
        in_specs=[pl.BlockSpec(memory_space=pltpu.SMEM)] + [anywhere] * 8,
        out_specs=(pl.BlockSpec(memory_space=pltpu.VMEM), anywhere),
        scratch_shapes=[
            pltpu.VMEM((rows, steps, width), BF16),
            pltpu.VMEM((rows, steps, HEAD_SIZE), BF16),
            pltpu.VMEM((rows, steps, both), BF16),
            pltpu.VMEM((rows, span, both), BF16),
            pltpu.VMEM((owned, width), BF16),
            pltpu.VMEM((1, width), F32),
            pltpu.VMEM((rank, n * owned), BF16),
            pltpu.VMEM((4 * n, rank, chunk), BF16),
            pltpu.VMEM((count, HEAD_SIZE), F32),
            pltpu.VMEM((count, both), F32),
            pltpu.VMEM((count, part), F32),
            pltpu.VMEM((2 * count, HEAD_SIZE), BF16),
            pltpu.VMEM((peers, 2 * count, HEAD_SIZE), BF16),
            pltpu.VMEM((peers, 2 * count, half), BF16),
            pltpu.VMEM((peers, 2 * count, half), BF16),
            pltpu.VMEM((count, 128), F32),
            pltpu.VMEM((peers, count, 128), F32),
            pltpu.VMEM((2 * count, half), BF16),
            pltpu.VMEM((peers, 2 * count, half), BF16),
            pltpu.VMEM((count, part), F32),
            pltpu.VMEM((count, part), F32),
            dma((8,)),
            dma((4 * n,)),
            dma((peers,)),
            dma((peers,)),
            dma((n,)),
            dma((n,)),
            dma((2 * n,)),
            dma((2 * n,)),
        ]
        + [dma((peers,))] * 10,
        compiler_params=pltpu.CompilerParams(
            collective_id=0, has_side_effects=True, vmem_limit_bytes=24 * 2**20
        ),
        cost_estimate=pl.CostEstimate(
            flops=2 * owned * width * (rank + count), bytes_accessed=6 * 2**20, transcendentals=0
        ),
    )(
        lengths,
        hidden,
        query,
        incoming_key_value.reshape(rows, steps, both),
        cache.reshape(rows, span, both),
        output_projection_weight,
        adapter_down_factor,
        adapter_up_factor.T,
        gain.reshape(1, width),
    )


def solution(mesh):
    fits = mesh.shape["tensor"] == 4 and mesh.shape["replica"] == 4
    return jax.shard_map(
        fused if fits else per_device,
        mesh=mesh,
        in_specs=(
            P(("groups", "replica"), None, None),
            P(("groups", "replica"), None, "tensor"),
            P(("groups", "replica"), None, "tensor", None),
            P(("groups", "replica"), None, "tensor", None),
            P(("groups", "replica")),
            P("tensor", None),
            P(("groups", "tensor"), None),
            P(("groups", "tensor", "replica"), None),
            P(),
        ),
        out_specs=(P(("groups", "replica"), None, None), P(("groups", "tensor"), None)),
        check_vma=False,
    )
```

```python
import functools
import math

import jax
import jax.numpy as jnp
from jax import lax
from jax.experimental import pallas as pl
from jax.experimental.pallas import tpu as pltpu
from jax.sharding import PartitionSpec as P

HEAD_SIZE = 128


ADAPTER_SCALE = 2.0
EPS = 1e-06


def attend(query, incoming_key_value, cache, lengths):
    row_count, steps, features = query.shape
    heads = features // HEAD_SIZE
    span = cache.shape[1]
    queries = query.reshape(row_count, steps, heads, HEAD_SIZE)
    scale_factor = 1.0 / math.sqrt(HEAD_SIZE)
    older = (
        jnp.einsum(
            "rihd,rlhd->rihl", queries, cache[..., :HEAD_SIZE], preferred_element_type=jnp.float32
        )
        * scale_factor
    )
    fresh = (
        jnp.einsum(
            "rihd,rjhd->rihj",
            queries,
            incoming_key_value[..., :HEAD_SIZE],
            preferred_element_type=jnp.float32,
        )
        * scale_factor
    )
    live_old = jnp.arange(span, dtype=jnp.int32)[None, None, None, :] < lengths[:, None, None, None]
    live_new = (
        jnp.arange(steps, dtype=jnp.int32)[None, None, None, :]
        <= jnp.arange(steps, dtype=jnp.int32)[None, :, None, None]
    )
    scores = jnp.concatenate(
        [jnp.where(live_old, older, -1e30), jnp.where(live_new, fresh, -1e30)], axis=3
    )
    weights = jax.nn.softmax(scores, axis=3).astype(jnp.bfloat16)
    mixed = jnp.einsum(
        "rihl,rlhd->rihd",
        weights[..., :span],
        cache[..., HEAD_SIZE:],
        preferred_element_type=jnp.float32,
    )
    mixed = mixed + jnp.einsum(
        "rihj,rjhd->rihd",
        weights[..., span:],
        incoming_key_value[..., HEAD_SIZE:],
        preferred_element_type=jnp.float32,
    )
    return mixed.astype(jnp.bfloat16).reshape(row_count, steps, features)


def per_device(
    hidden,
    query,
    incoming_key_value,
    cache,
    lengths,
    output_projection_weight,
    adapter_down_factor,
    adapter_up_factor,
    gain,
):
    context = attend(query, incoming_key_value, cache, lengths)
    owned = output_projection_weight.shape[0]
    complete_down_factor = lax.all_gather(adapter_down_factor, "tensor", axis=0, tiled=True)
    a_columns = lax.dynamic_slice_in_dim(
        complete_down_factor, lax.axis_index("tensor") * owned, owned, 1
    )
    adapter_update = lax.dot_general(
        a_columns,
        lax.all_gather(adapter_up_factor, ("tensor", "replica"), axis=0, tiled=True),
        (((0,), (1,)), ((), ())),
        preferred_element_type=jnp.float32,
    )
    merged = (output_projection_weight.astype(jnp.float32) + ADAPTER_SCALE * adapter_update).astype(
        jnp.bfloat16
    )
    row_count, steps = (context.shape[0], context.shape[1])
    partial_value = jnp.dot(
        context.reshape(row_count * steps, owned), merged, preferred_element_type=jnp.float32
    )
    partial_value = partial_value.reshape(row_count, steps, merged.shape[1])
    summed = lax.psum(partial_value, "tensor")
    resid = hidden.astype(jnp.float32) + summed
    mean_square = jnp.mean(resid * resid, axis=-1, keepdims=True)
    normed = (resid * lax.rsqrt(mean_square + EPS) * gain).astype(jnp.bfloat16)
    return (normed, merged)


MESH = pl.DeviceIdType.MESH
F32 = jnp.float32
BF16 = jnp.bfloat16


def fused_kernel(
    sizes,
    lengths_hbm,
    hidden_hbm,
    query_hbm,
    fresh_hbm,
    cache_hbm,
    weight_hbm,
    down_hbm,
    up_hbm,
    gain_hbm,
    normed_ref,
    merged_ref,
    lengths_ref,
    hidden_ref,
    query_ref,
    fresh_ref,
    cache_ref,
    weight_ref,
    gain_ref,
    down_all,
    up_all,
    queries,
    fresh_rows,
    hidden_rows,
    context_out,
    context_in,
    part_out,
    part_in,
    square_out,
    square_in,
    resid_out,
    resid_in,
    own_sum,
    own_resid,
    load_sem,
    z_send,
    z_recv,
    x_send,
    x_recv,
    c_send,
    c_recv,
    a_send,
    a_recv,
    ctx_send,
    ctx_recv,
    rs_send,
    rs_recv,
    sq_send,
    sq_recv,
    ag_send,
    ag_recv,
):
    rows, steps, span, width, owned, n = sizes
    count = rows * steps
    part = width // n
    half = part // 2
    chunk = up_hbm.shape[1]
    rank_part = down_hbm.shape[0]
    t = lax.axis_index("tensor")
    r = lax.axis_index("replica")
    across = lax.rem(r + 2, 4)
    beside = r + 1 - 2 * lax.rem(r, 2)
    me = t * 4 + r

    def ahead(k):
        return lax.rem(t + k, n)

    def behind(k):
        return lax.rem(t + n - k, n)

    def remote(source, target, send, recv, device):
        return pltpu.make_async_remote_copy(
            src_ref=source,
            dst_ref=target,
            send_sem=send,
            recv_sem=recv,
            device_id=device,
            device_id_type=MESH,
        )

    mine = pl.ds(pl.multiple_of(t * rank_part, rank_part), rank_part)
    loads = [
        pltpu.make_async_copy(a, b, load_sem.at[i])
        for i, (a, b) in enumerate(
            [
                (up_hbm, up_all.at[me]),
                (down_hbm, down_all.at[mine]),
                (query_hbm, query_ref),
                (fresh_hbm, fresh_ref),
                (cache_hbm, cache_ref),
                (weight_hbm, weight_ref),
                (hidden_hbm, hidden_ref),
                (gain_hbm, gain_ref),
                (lengths_hbm, lengths_ref),
            ]
        )
    ]
    for load in loads:
        load.start()

    barrier = pltpu.get_barrier_semaphore()
    for k in range(1, n):
        pl.semaphore_signal(barrier, inc=1, device_id={"tensor": ahead(k)}, device_id_type=MESH)
    pl.semaphore_signal(barrier, inc=1, device_id={"replica": across}, device_id_type=MESH)
    pl.semaphore_signal(barrier, inc=1, device_id={"replica": beside}, device_id_type=MESH)

    z_copies = [
        remote(up_all.at[me], up_all.at[me], z_send.at[k - 1], z_recv.at[k - 1], {"tensor": ahead(k)})
        for k in range(1, n)
    ]
    x_copies = []
    c_copies = []
    for k in range(n):
        near = behind(k) * 4 + r
        far = behind(k) * 4 + across
        x_copies.append(
            remote(up_all.at[near], up_all.at[near], x_send.at[k], x_recv.at[k], {"replica": across})
        )
        for j, slot in enumerate((near, far)):
            i = 2 * k + j
            c_copies.append(
                remote(up_all.at[slot], up_all.at[slot], c_send.at[i], c_recv.at[i], {"replica": beside})
            )
    a_copies = [
        remote(
            down_all.at[mine], down_all.at[mine], a_send.at[k - 1], a_recv.at[k - 1], {"tensor": ahead(k)}
        )
        for k in range(1, n)
    ]

    loads[0].wait()
    loads[1].wait()
    pl.semaphore_wait(barrier, n + 1)
    x_copies[0].start()
    c_copies[0].start()
    for k in (2, 1, 3):
        z_copies[k - 1].start()
    for copy in a_copies:
        copy.start()

    loads[2].wait()
    loads[3].wait()
    for i in range(rows):
        queries[i * steps : (i + 1) * steps, :] = query_ref[i].astype(F32)
        fresh_rows[i * steps : (i + 1) * steps, :] = fresh_ref[i].astype(F32)
    q = queries[...].astype(BF16)
    fresh = fresh_rows[...].astype(BF16)
    scale_factor = 1.0 / math.sqrt(HEAD_SIZE)
    contract = (((1,), (1,)), ((), ()))
    loads[4].wait()
    loads[8].wait()
    keys = cache_ref[:, :, :HEAD_SIZE].reshape(rows * span, HEAD_SIZE)
    values = cache_ref[:, :, HEAD_SIZE:].reshape(rows * span, HEAD_SIZE)
    older = lax.dot_general(q, keys, contract, preferred_element_type=F32) * scale_factor
    newer = lax.dot_general(
        q, fresh[:, :HEAD_SIZE], contract, preferred_element_type=F32
    ) * scale_factor
    row = lax.broadcasted_iota(jnp.int32, (count, rows * span), 0)
    column = lax.broadcasted_iota(jnp.int32, (count, rows * span), 1)
    low = (row // steps) * span
    high = low
    for i in range(rows):
        high = jnp.where(row // steps == i, i * span + lengths_ref[i], high)
    older = jnp.where((column >= low) & (column < high), older, -1e30)
    row = lax.broadcasted_iota(jnp.int32, (count, count), 0)
    column = lax.broadcasted_iota(jnp.int32, (count, count), 1)
    keep = (row // steps == column // steps) & (column <= row)
    newer = jnp.where(keep, newer, -1e30)
    top = jnp.maximum(
        jnp.max(older, axis=1, keepdims=True), jnp.max(newer, axis=1, keepdims=True)
    )
    older = jnp.exp(older - top)
    newer = jnp.exp(newer - top)
    total = jnp.sum(older, axis=1, keepdims=True) + jnp.sum(newer, axis=1, keepdims=True)
    older = (older / total).astype(BF16)
    newer = (newer / total).astype(BF16)
    context = jnp.dot(older, values, preferred_element_type=F32)
    context = context + jnp.dot(newer, fresh[:, HEAD_SIZE:], preferred_element_type=F32)
    context16 = jnp.concatenate([context, jnp.zeros_like(context)], axis=0).astype(BF16)
    context_out[...] = context16
    ctx_copies = [
        remote(
            context_out,
            context_in.at[k - 1],
            ctx_send.at[k - 1],
            ctx_recv.at[k - 1],
            {"tensor": ahead(k)},
        )
        for k in range(1, n)
    ]
    for copy in ctx_copies:
        copy.start()

    def columns(owner):
        return pl.ds(pl.multiple_of(owner * part, part), part)

    context = context_out[...]
    loads[5].wait()
    rs_copies = [None] * n
    for k in (2, 1, 3):
        product = jnp.dot(context, weight_ref[:, columns(ahead(k))], preferred_element_type=F32)
        part_out[k - 1] = jnp.concatenate(
            [product[:count, :half], product[:count, half:]], axis=0
        ).astype(BF16)
        rs_copies[k] = remote(
            part_out.at[k - 1],
            part_in.at[k - 1],
            rs_send.at[k - 1],
            rs_recv.at[k - 1],
            {"tensor": ahead(k)},
        )
        rs_copies[k].start()
    x_copies[0].wait_recv()
    c_copies[1].start()
    for k in range(1, n):
        z_copies[k - 1].wait_recv()
        x_copies[k].start()
        c_copies[2 * k].start()
    loads[6].wait()
    for i in range(rows):
        hidden_rows[i * steps : (i + 1) * steps, :] = hidden_ref[i, :, columns(t)].astype(F32)
    product = jnp.dot(context, weight_ref[:, columns(t)], preferred_element_type=F32)
    own_sum[...] = product[:count] + hidden_rows[...]

    for copy in a_copies:
        copy.wait_recv()
    head = pl.ds(pl.multiple_of(t * owned, owned), owned)
    own_down = (down_all[:, head].astype(F32) * ADAPTER_SCALE).T.astype(BF16)

    def merge(slot):
        place = pl.ds(pl.multiple_of(slot * chunk, chunk), chunk)
        update = jnp.dot(own_down, up_all[slot], preferred_element_type=F32)
        merged_ref[:, place] = (weight_ref[:, place].astype(F32) + update).astype(BF16)

    for k in range(n):
        merge(behind(k) * 4 + r)

    for copy in ctx_copies:
        copy.wait_recv()
    inner = jnp.dot(context, own_down, preferred_element_type=F32)
    for k in range(1, n):
        other = pl.ds(pl.multiple_of(behind(k) * owned, owned), owned)
        inner = inner + ADAPTER_SCALE * lax.dot_general(
            context_in[k - 1], down_all[:, other], contract, preferred_element_type=F32
        )
    inner = inner[:count]
    upper = inner.astype(BF16).astype(F32)
    inner = jnp.concatenate([upper, inner - upper], axis=0).astype(BF16)
    c_copies[0].wait_recv()
    c_copies[1].wait_recv()
    for k in range(1, n):
        rs_copies[k].wait_recv()
    squares = jnp.zeros((count, 1), F32)
    pieces = []
    for j in range(4):
        place = slice(j * chunk, (j + 1) * chunk)
        term = jnp.dot(inner, up_all[t * 4 + j], preferred_element_type=F32)
        value = own_sum[:, place] + term[:count] + term[count:]
        for k in range(1, n):
            top_rows = (j * chunk) // half * count
            start = (j * chunk) % half
            value = value + part_in[k - 1, :, start : start + chunk].astype(F32)[
                top_rows : top_rows + count
            ]
        squares = squares + jnp.sum(value * value, axis=1, keepdims=True)
        own_resid[:, place] = value
        pieces.append(value)
    square_out[...] = jnp.broadcast_to(squares, square_out.shape)
    resid_out[...] = jnp.concatenate(
        [
            jnp.concatenate([pieces[0], pieces[1]], axis=1),
            jnp.concatenate([pieces[2], pieces[3]], axis=1),
        ],
        axis=0,
    ).astype(BF16)
    ag_copies = []
    for k in (2, 1, 3):
        device = {"tensor": ahead(k)}
        copies = [
            remote(square_out, square_in.at[k - 1], sq_send.at[k - 1], sq_recv.at[k - 1], device),
            remote(resid_out, resid_in.at[k - 1], ag_send.at[k - 1], ag_recv.at[k - 1], device),
        ]
        for copy in copies:
            copy.start()
        ag_copies.append((k, copies))

    for k in range(1, n):
        x_copies[k].wait_recv()
        c_copies[2 * k + 1].start()
    for k in range(n):
        merge(behind(k) * 4 + across)
    opposite = lax.rem(beside + 2, 4)
    for k in range(n):
        if k:
            c_copies[2 * k].wait_recv()
        merge(behind(k) * 4 + beside)
    for k in range(n):
        if k:
            c_copies[2 * k + 1].wait_recv()
        merge(behind(k) * 4 + opposite)

    for k, copies in ag_copies:
        copies[0].wait_recv()
        squares = squares + square_in[k - 1, :, :1]
    factor = lax.rsqrt(squares / width + EPS)
    loads[7].wait()
    value = own_resid[...] * factor * gain_ref[:, columns(t)]
    for i in range(rows):
        normed_ref[i, :, columns(t)] = value[i * steps : (i + 1) * steps].astype(BF16)
    for k, copies in ag_copies:
        copies[1].wait_recv()
        arrived = resid_in[k - 1].astype(F32)
        value = jnp.concatenate([arrived[:count], arrived[count:]], axis=1)
        place = columns(behind(k))
        value = value * factor * gain_ref[:, place]
        for i in range(rows):
            normed_ref[i, :, place] = value[i * steps : (i + 1) * steps].astype(BF16)

    for copy in z_copies + x_copies + c_copies + a_copies + ctx_copies + rs_copies[1:]:
        copy.wait_send()
    for k, copies in ag_copies:
        for copy in copies:
            copy.wait_send()


def store_kernel(normed_ref, merged_ref, normed_hbm, merged_hbm, sem):
    step = merged_ref.shape[0] // 8
    copies = [
        pltpu.make_async_copy(
            merged_ref.at[i * step : (i + 1) * step], merged_hbm.at[i * step : (i + 1) * step], sem.at[i]
        )
        for i in range(8)
    ]
    copies.append(pltpu.make_async_copy(normed_ref, normed_hbm, sem.at[8]))
    for copy in copies:
        copy.start()
    for copy in copies:
        copy.wait()


def fused(
    hidden,
    query,
    incoming_key_value,
    cache,
    lengths,
    output_projection_weight,
    adapter_down_factor,
    adapter_up_factor,
    gain,
):
    rows, steps, width = hidden.shape
    span = cache.shape[1]
    owned = output_projection_weight.shape[0]
    n = adapter_down_factor.shape[1] // owned
    rank = adapter_up_factor.shape[1]
    chunk = adapter_up_factor.shape[0]
    count = rows * steps
    part = width // n
    half = part // 2
    both = 2 * HEAD_SIZE
    outside = pl.BlockSpec(memory_space=pltpu.HBM)
    inside = pl.BlockSpec(memory_space=pltpu.VMEM)
    dma = pltpu.SemaphoreType.DMA
    peers = n - 1
    normed, merged = pl.pallas_call(
        functools.partial(fused_kernel, (rows, steps, span, width, owned, n)),
        out_shape=(
            jax.ShapeDtypeStruct((rows, steps, width), BF16),
            jax.ShapeDtypeStruct((owned, width), BF16),
        ),
        in_specs=[outside] * 9,
        out_specs=(inside, inside),
        scratch_shapes=[
            pltpu.SMEM((rows,), jnp.int32),
            pltpu.VMEM((rows, steps, width), BF16),
            pltpu.VMEM((rows, steps, HEAD_SIZE), BF16),
            pltpu.VMEM((rows, steps, both), BF16),
            pltpu.VMEM((rows, span, both), BF16),
            pltpu.VMEM((owned, width), BF16),
            pltpu.VMEM((1, width), F32),
            pltpu.VMEM((rank, n * owned), BF16),
            pltpu.VMEM((4 * n, rank, chunk), BF16),
            pltpu.VMEM((count, HEAD_SIZE), F32),
            pltpu.VMEM((count, both), F32),
            pltpu.VMEM((count, part), F32),
            pltpu.VMEM((2 * count, HEAD_SIZE), BF16),
            pltpu.VMEM((peers, 2 * count, HEAD_SIZE), BF16),
            pltpu.VMEM((peers, 2 * count, half), BF16),
            pltpu.VMEM((peers, 2 * count, half), BF16),
            pltpu.VMEM((count, 128), F32),
            pltpu.VMEM((peers, count, 128), F32),
            pltpu.VMEM((2 * count, half), BF16),
            pltpu.VMEM((peers, 2 * count, half), BF16),
            pltpu.VMEM((count, part), F32),
            pltpu.VMEM((count, part), F32),
            dma((9,)),
            dma((peers,)),
            dma((peers,)),
            dma((n,)),
            dma((n,)),
            dma((2 * n,)),
            dma((2 * n,)),
        ]
        + [dma((peers,))] * 10,
        compiler_params=pltpu.CompilerParams(
            collective_id=0, has_side_effects=True, vmem_limit_bytes=16 * 2**20
        ),
        cost_estimate=pl.CostEstimate(
            flops=2 * owned * width * (rank + count), bytes_accessed=6 * 2**20, transcendentals=0
        ),
    )(
        *[
            pltpu.with_memory_space_constraint(operand, pltpu.HBM)
            for operand in (
                lengths,
                hidden,
                query,
                incoming_key_value.reshape(rows, steps, both),
                cache.reshape(rows, span, both),
                output_projection_weight,
                adapter_down_factor,
                adapter_up_factor.T,
                gain.reshape(1, width),
            )
        ]
    )
    return pl.pallas_call(
        store_kernel,
        out_shape=(
            jax.ShapeDtypeStruct(normed.shape, BF16),
            jax.ShapeDtypeStruct(merged.shape, BF16),
        ),
        in_specs=[inside, inside],
        out_specs=(outside, outside),
        scratch_shapes=[dma((9,))],
        compiler_params=pltpu.CompilerParams(vmem_limit_bytes=16 * 2**20),
    )(normed, merged)


def solution(mesh):
    fits = mesh.shape["tensor"] == 4 and mesh.shape["replica"] == 4
    return jax.shard_map(
        fused if fits else per_device,
        mesh=mesh,
        in_specs=(
            P(("groups", "replica"), None, None),
            P(("groups", "replica"), None, "tensor"),
            P(("groups", "replica"), None, "tensor", None),
            P(("groups", "replica"), None, "tensor", None),
            P(("groups", "replica")),
            P("tensor", None),
            P(("groups", "tensor"), None),
            P(("groups", "tensor", "replica"), None),
            P(),
        ),
        out_specs=(P(("groups", "replica"), None, None), P(("groups", "tensor"), None)),
        check_vma=False,
    )
```

```python
import functools
import math

import jax
import jax.numpy as jnp
from jax import lax
from jax.experimental import pallas as pl
from jax.experimental.pallas import tpu as pltpu
from jax.sharding import PartitionSpec as P

HEAD_SIZE = 128


ADAPTER_SCALE = 2.0
EPS = 1e-06


def attend(query, incoming_key_value, cache, lengths):
    row_count, steps, features = query.shape
    heads = features // HEAD_SIZE
    span = cache.shape[1]
    queries = query.reshape(row_count, steps, heads, HEAD_SIZE)
    scale_factor = 1.0 / math.sqrt(HEAD_SIZE)
    older = (
        jnp.einsum(
            "rihd,rlhd->rihl", queries, cache[..., :HEAD_SIZE], preferred_element_type=jnp.float32
        )
        * scale_factor
    )
    fresh = (
        jnp.einsum(
            "rihd,rjhd->rihj",
            queries,
            incoming_key_value[..., :HEAD_SIZE],
            preferred_element_type=jnp.float32,
        )
        * scale_factor
    )
    live_old = jnp.arange(span, dtype=jnp.int32)[None, None, None, :] < lengths[:, None, None, None]
    live_new = (
        jnp.arange(steps, dtype=jnp.int32)[None, None, None, :]
        <= jnp.arange(steps, dtype=jnp.int32)[None, :, None, None]
    )
    scores = jnp.concatenate(
        [jnp.where(live_old, older, -1e30), jnp.where(live_new, fresh, -1e30)], axis=3
    )
    weights = jax.nn.softmax(scores, axis=3).astype(jnp.bfloat16)
    mixed = jnp.einsum(
        "rihl,rlhd->rihd",
        weights[..., :span],
        cache[..., HEAD_SIZE:],
        preferred_element_type=jnp.float32,
    )
    mixed = mixed + jnp.einsum(
        "rihj,rjhd->rihd",
        weights[..., span:],
        incoming_key_value[..., HEAD_SIZE:],
        preferred_element_type=jnp.float32,
    )
    return mixed.astype(jnp.bfloat16).reshape(row_count, steps, features)


def per_device(
    hidden,
    query,
    incoming_key_value,
    cache,
    lengths,
    output_projection_weight,
    adapter_down_factor,
    adapter_up_factor,
    gain,
):
    context = attend(query, incoming_key_value, cache, lengths)
    owned = output_projection_weight.shape[0]
    complete_down_factor = lax.all_gather(adapter_down_factor, "tensor", axis=0, tiled=True)
    a_columns = lax.dynamic_slice_in_dim(
        complete_down_factor, lax.axis_index("tensor") * owned, owned, 1
    )
    adapter_update = lax.dot_general(
        a_columns,
        lax.all_gather(adapter_up_factor, ("tensor", "replica"), axis=0, tiled=True),
        (((0,), (1,)), ((), ())),
        preferred_element_type=jnp.float32,
    )
    merged = (output_projection_weight.astype(jnp.float32) + ADAPTER_SCALE * adapter_update).astype(
        jnp.bfloat16
    )
    row_count, steps = (context.shape[0], context.shape[1])
    partial_value = jnp.dot(
        context.reshape(row_count * steps, owned), merged, preferred_element_type=jnp.float32
    )
    partial_value = partial_value.reshape(row_count, steps, merged.shape[1])
    summed = lax.psum(partial_value, "tensor")
    resid = hidden.astype(jnp.float32) + summed
    mean_square = jnp.mean(resid * resid, axis=-1, keepdims=True)
    normed = (resid * lax.rsqrt(mean_square + EPS) * gain).astype(jnp.bfloat16)
    return (normed, merged)


MESH = pl.DeviceIdType.MESH
F32 = jnp.float32
BF16 = jnp.bfloat16
PIECES = 2


def fused_kernel(
    sizes,
    lengths_hbm,
    hidden_hbm,
    query_hbm,
    fresh_hbm,
    cache_hbm,
    weight_hbm,
    down_hbm,
    up_hbm,
    gain_hbm,
    normed_ref,
    merged_ref,
    lengths_ref,
    hidden_ref,
    query_ref,
    fresh_ref,
    cache_ref,
    weight_ref,
    gain_ref,
    down_all,
    up_all,
    queries,
    fresh_rows,
    hidden_rows,
    context_out,
    context_in,
    part_out,
    part_in,
    square_out,
    square_in,
    resid_out,
    resid_in,
    own_sum,
    own_resid,
    load_sem,
    z_send,
    z_recv,
    x_send,
    x_recv,
    c_send,
    c_recv,
    a_send,
    a_recv,
    ctx_send,
    ctx_recv,
    rs_send,
    rs_recv,
    sq_send,
    sq_recv,
    ag_send,
    ag_recv,
):
    rows, steps, span, width, owned, n = sizes
    count = rows * steps
    part = width // n
    half = part // 2
    chunk = up_hbm.shape[1]
    rank_part = down_hbm.shape[0]
    t = lax.axis_index("tensor")
    r = lax.axis_index("replica")
    across = lax.rem(r + 2, 4)
    beside = r + 1 - 2 * lax.rem(r, 2)
    me = t * 4 + r

    def ahead(k):
        return lax.rem(t + k, n)

    def behind(k):
        return lax.rem(t + n - k, n)

    def remote(source, target, send, recv, device):
        return pltpu.make_async_remote_copy(
            src_ref=source,
            dst_ref=target,
            send_sem=send,
            recv_sem=recv,
            device_id=device,
            device_id_type=MESH,
        )

    def gather(source, slot, send, recv, device):
        depth = up_hbm.shape[0] // PIECES
        copies = []
        for p in range(PIECES):
            piece = slice(p * depth, (p + 1) * depth)
            copies.append(
                remote(
                    source.at[piece], up_all.at[slot, piece], send.at[p], recv.at[p], device
                )
            )
        return copies

    mine = pl.ds(pl.multiple_of(t * rank_part, rank_part), rank_part)
    loads = [
        pltpu.make_async_copy(a, b, load_sem.at[i])
        for i, (a, b) in enumerate(
            [
                (up_hbm, up_all.at[me]),
                (down_hbm, down_all.at[mine]),
                (query_hbm, query_ref),
                (fresh_hbm, fresh_ref),
                (cache_hbm, cache_ref),
                (weight_hbm, weight_ref),
                (hidden_hbm, hidden_ref),
                (gain_hbm, gain_ref),
                (lengths_hbm, lengths_ref),
            ]
        )
    ]
    for load in loads:
        load.start()

    barrier = pltpu.get_barrier_semaphore()
    for k in range(1, n):
        pl.semaphore_signal(barrier, inc=1, device_id={"tensor": ahead(k)}, device_id_type=MESH)
    pl.semaphore_signal(barrier, inc=1, device_id={"replica": across}, device_id_type=MESH)
    pl.semaphore_signal(barrier, inc=1, device_id={"replica": beside}, device_id_type=MESH)

    side = t // 2
    inside = (t == 1) | (t == 2)
    mate = t + 1 - 2 * lax.rem(t, 2)
    sources = [t, mate, 2 - side, 3 - 3 * side]
    nears = [source * 4 + r for source in sources]
    fars = [source * 4 + across for source in sources]
    landing = 1 + lax.rem(t + side + 1, 2)
    z_copies = [
        gather(up_all.at[me], me, z_send.at[0], z_recv.at[0], {"tensor": mate}),
        gather(up_all.at[me], me, z_send.at[1], z_recv.at[landing], {"tensor": 2 - side}),
    ]
    passed = [
        gather(up_all.at[nears[k]], nears[k], z_send.at[k], z_recv.at[k - 1], {"tensor": mate})
        for k in (2, 3)
    ]
    z_arrivals = [
        gather(up_all.at[nears[k]], nears[k], z_send.at[0], z_recv.at[k - 1], {"tensor": mate})
        for k in (1, 2, 3)
    ]
    x_copies = []
    c_copies = []
    for k in range(n):
        x_copies.append(
            gather(up_all.at[nears[k]], nears[k], x_send.at[k], x_recv.at[k], {"replica": across})
        )
        for j, slot in enumerate((nears[k], fars[k])):
            i = 2 * k + j
            c_copies.append(
                gather(up_all.at[slot], slot, c_send.at[i], c_recv.at[i], {"replica": beside})
            )
    a_copies = [
        remote(
            down_all.at[mine], down_all.at[mine], a_send.at[k - 1], a_recv.at[k - 1], {"tensor": ahead(k)}
        )
        for k in range(1, n)
    ]

    loads[0].wait()
    loads[1].wait()
    pl.semaphore_wait(barrier, n + 1)
    for p in range(PIECES):
        for copies in z_copies:
            copies[p].start()
        x_copies[0][p].start()
        c_copies[0][p].start()
    for copy in a_copies:
        copy.start()

    loads[2].wait()
    loads[3].wait()
    for i in range(rows):
        queries[i * steps : (i + 1) * steps, :] = query_ref[i].astype(F32)
        fresh_rows[i * steps : (i + 1) * steps, :] = fresh_ref[i].astype(F32)
    q = queries[...].astype(BF16)
    fresh = fresh_rows[...].astype(BF16)
    scale_factor = 1.0 / math.sqrt(HEAD_SIZE)
    contract = (((1,), (1,)), ((), ()))
    loads[4].wait()
    loads[8].wait()
    keys = cache_ref[:, :, :HEAD_SIZE].reshape(rows * span, HEAD_SIZE)
    values = cache_ref[:, :, HEAD_SIZE:].reshape(rows * span, HEAD_SIZE)
    older = lax.dot_general(q, keys, contract, preferred_element_type=F32) * scale_factor
    newer = lax.dot_general(
        q, fresh[:, :HEAD_SIZE], contract, preferred_element_type=F32
    ) * scale_factor
    row = lax.broadcasted_iota(jnp.int32, (count, rows * span), 0)
    column = lax.broadcasted_iota(jnp.int32, (count, rows * span), 1)
    low = (row // steps) * span
    high = low
    for i in range(rows):
        high = jnp.where(row // steps == i, i * span + lengths_ref[i], high)
    older = jnp.where((column >= low) & (column < high), older, -1e30)
    row = lax.broadcasted_iota(jnp.int32, (count, count), 0)
    column = lax.broadcasted_iota(jnp.int32, (count, count), 1)
    keep = (row // steps == column // steps) & (column <= row)
    newer = jnp.where(keep, newer, -1e30)
    top = jnp.maximum(
        jnp.max(older, axis=1, keepdims=True), jnp.max(newer, axis=1, keepdims=True)
    )
    older = jnp.exp(older - top)
    newer = jnp.exp(newer - top)
    total = jnp.sum(older, axis=1, keepdims=True) + jnp.sum(newer, axis=1, keepdims=True)
    older = (older / total).astype(BF16)
    newer = (newer / total).astype(BF16)
    context = jnp.dot(older, values, preferred_element_type=F32)
    context = context + jnp.dot(newer, fresh[:, HEAD_SIZE:], preferred_element_type=F32)
    context16 = jnp.concatenate([context, jnp.zeros_like(context)], axis=0).astype(BF16)
    context_out[...] = context16
    ctx_copies = [
        remote(
            context_out,
            context_in.at[k - 1],
            ctx_send.at[k - 1],
            ctx_recv.at[k - 1],
            {"tensor": ahead(k)},
        )
        for k in range(1, n)
    ]
    for copy in ctx_copies:
        copy.start()

    def columns(owner):
        return pl.ds(pl.multiple_of(owner * part, part), part)

    context = context_out[...]
    loads[5].wait()
    rs_copies = {}
    for h in range(2):
        for k in (2, 1, 3):
            place = pl.ds(pl.multiple_of(ahead(k) * part + h * half, half), half)
            product = jnp.dot(context, weight_ref[:, place], preferred_element_type=F32)
            i = 2 * (k - 1) + h
            part_out[i] = jnp.concatenate(
                [product[:count, :chunk], product[:count, chunk:]], axis=0
            ).astype(BF16)
            rs_copies[h, k] = remote(
                part_out.at[i], part_in.at[i], rs_send.at[i], rs_recv.at[i], {"tensor": ahead(k)}
            )
            rs_copies[h, k].start()
    for p in range(PIECES):
        x_copies[0][p].wait_recv()
        c_copies[1][p].start()
    for p in range(PIECES):
        z_arrivals[0][p].wait_recv()
        x_copies[1][p].start()
        c_copies[2][p].start()

    def spread(forward):
        for k in (2, 3):
            for p in range(PIECES):
                z_arrivals[k - 1][p].wait_recv()
                if forward:
                    passed[k - 2][p].start()
                x_copies[k][p].start()
                c_copies[2 * k][p].start()

    pl.when(inside)(lambda: spread(True))
    loads[6].wait()
    for i in range(rows):
        hidden_rows[i * steps : (i + 1) * steps, :] = hidden_ref[i, :, columns(t)].astype(F32)
    product = jnp.dot(context, weight_ref[:, columns(t)], preferred_element_type=F32)
    own_sum[...] = product[:count] + hidden_rows[...]

    for copy in a_copies:
        copy.wait_recv()
    head = pl.ds(pl.multiple_of(t * owned, owned), owned)
    own_down = (down_all[:, head].astype(F32) * ADAPTER_SCALE).T.astype(BF16)

    def merge(slot):
        place = pl.ds(pl.multiple_of(slot * chunk, chunk), chunk)
        update = jnp.dot(own_down, up_all[slot], preferred_element_type=F32)
        merged_ref[:, place] = (weight_ref[:, place].astype(F32) + update).astype(BF16)

    for copy in ctx_copies:
        copy.wait_recv()
    inner = jnp.dot(context, own_down, preferred_element_type=F32)
    for k in range(1, n):
        other = pl.ds(pl.multiple_of(behind(k) * owned, owned), owned)
        inner = inner + ADAPTER_SCALE * lax.dot_general(
            context_in[k - 1], down_all[:, other], contract, preferred_element_type=F32
        )
    inner = inner[:count]
    upper = inner.astype(BF16).astype(F32)
    inner = jnp.concatenate([upper, inner - upper], axis=0).astype(BF16)
    for copy in c_copies[0] + c_copies[1]:
        copy.wait_recv()
    squares = jnp.zeros((count, 1), F32)
    ag_copies = []
    sq_copies = []
    for h in range(2):
        for k in range(1, n):
            rs_copies[h, k].wait_recv()
        pieces = []
        for j in range(2):
            place = slice((2 * h + j) * chunk, (2 * h + j + 1) * chunk)
            term = jnp.dot(inner, up_all[t * 4 + 2 * h + j], preferred_element_type=F32)
            value = own_sum[:, place] + term[:count] + term[count:]
            for k in range(1, n):
                value = value + part_in[2 * (k - 1) + h].astype(F32)[j * count : (j + 1) * count]
            squares = squares + jnp.sum(value * value, axis=1, keepdims=True)
            own_resid[:, place] = value
            pieces.append(value)
        resid_out[h] = jnp.concatenate(pieces, axis=0).astype(BF16)
        if h:
            square_out[...] = jnp.broadcast_to(squares, square_out.shape)
        for k in (2, 1, 3):
            device = {"tensor": ahead(k)}
            i = 2 * (k - 1) + h
            if h:
                copy = remote(
                    square_out, square_in.at[k - 1], sq_send.at[k - 1], sq_recv.at[k - 1], device
                )
                copy.start()
                sq_copies.append(copy)
            copy = remote(resid_out.at[h], resid_in.at[i], ag_send.at[i], ag_recv.at[i], device)
            copy.start()
            ag_copies.append((h, k, copy))
        if not h:
            for p in range(PIECES):
                x_copies[1][p].wait_recv()
                c_copies[3][p].start()

    pl.when(jnp.logical_not(inside))(lambda: spread(False))
    for k in range(n):
        merge(nears[k])

    for k in range(2, n):
        for p in range(PIECES):
            x_copies[k][p].wait_recv()
            c_copies[2 * k + 1][p].start()
    for k in range(n):
        merge(fars[k])
    opposite = lax.rem(beside + 2, 4)
    for k in range(n):
        if k:
            for copy in c_copies[2 * k]:
                copy.wait_recv()
        merge(sources[k] * 4 + beside)
    for k in range(n):
        if k:
            for copy in c_copies[2 * k + 1]:
                copy.wait_recv()
        merge(sources[k] * 4 + opposite)

    for copy in sq_copies:
        copy.wait_recv()
    for k in range(1, n):
        squares = squares + square_in[k - 1, :, :1]
    factor = lax.rsqrt(squares / width + EPS)
    loads[7].wait()
    value = own_resid[...] * factor * gain_ref[:, columns(t)]
    for i in range(rows):
        normed_ref[i, :, columns(t)] = value[i * steps : (i + 1) * steps].astype(BF16)
    for h, k, copy in ag_copies:
        copy.wait_recv()
        arrived = resid_in[2 * (k - 1) + h].astype(F32)
        value = jnp.concatenate([arrived[:count], arrived[count:]], axis=1)
        place = pl.ds(pl.multiple_of(behind(k) * part + h * half, half), half)
        value = value * factor * gain_ref[:, place]
        for i in range(rows):
            normed_ref[i, :, place] = value[i * steps : (i + 1) * steps].astype(BF16)

    for copy in passed[0] + passed[1]:
        pl.when(inside)(copy.wait_send)
    for copies in z_copies + x_copies + c_copies:
        for copy in copies:
            copy.wait_send()
    for copy in a_copies + ctx_copies + sq_copies:
        copy.wait_send()
    for copy in rs_copies.values():
        copy.wait_send()
    for h, k, copy in ag_copies:
        copy.wait_send()


def store_kernel(normed_ref, merged_ref, normed_hbm, merged_hbm, sem):
    step = merged_ref.shape[0] // 8
    copies = [
        pltpu.make_async_copy(
            merged_ref.at[i * step : (i + 1) * step], merged_hbm.at[i * step : (i + 1) * step], sem.at[i]
        )
        for i in range(8)
    ]
    copies.append(pltpu.make_async_copy(normed_ref, normed_hbm, sem.at[8]))
    for copy in copies:
        copy.start()
    for copy in copies:
        copy.wait()


def fused(
    hidden,
    query,
    incoming_key_value,
    cache,
    lengths,
    output_projection_weight,
    adapter_down_factor,
    adapter_up_factor,
    gain,
):
    rows, steps, width = hidden.shape
    span = cache.shape[1]
    owned = output_projection_weight.shape[0]
    n = adapter_down_factor.shape[1] // owned
    rank = adapter_up_factor.shape[1]
    chunk = adapter_up_factor.shape[0]
    count = rows * steps
    part = width // n
    half = part // 2
    both = 2 * HEAD_SIZE
    outside = pl.BlockSpec(memory_space=pltpu.HBM)
    inside = pl.BlockSpec(memory_space=pltpu.VMEM)
    dma = pltpu.SemaphoreType.DMA
    peers = n - 1
    normed, merged = pl.pallas_call(
        functools.partial(fused_kernel, (rows, steps, span, width, owned, n)),
        out_shape=(
            jax.ShapeDtypeStruct((rows, steps, width), BF16),
            jax.ShapeDtypeStruct((owned, width), BF16),
        ),
        in_specs=[outside] * 9,
        out_specs=(inside, inside),
        scratch_shapes=[
            pltpu.SMEM((rows,), jnp.int32),
            pltpu.VMEM((rows, steps, width), BF16),
            pltpu.VMEM((rows, steps, HEAD_SIZE), BF16),
            pltpu.VMEM((rows, steps, both), BF16),
            pltpu.VMEM((rows, span, both), BF16),
            pltpu.VMEM((owned, width), BF16),
            pltpu.VMEM((1, width), F32),
            pltpu.VMEM((rank, n * owned), BF16),
            pltpu.VMEM((4 * n, rank, chunk), BF16),
            pltpu.VMEM((count, HEAD_SIZE), F32),
            pltpu.VMEM((count, both), F32),
            pltpu.VMEM((count, part), F32),
            pltpu.VMEM((2 * count, HEAD_SIZE), BF16),
            pltpu.VMEM((peers, 2 * count, HEAD_SIZE), BF16),
            pltpu.VMEM((2 * peers, 2 * count, chunk), BF16),
            pltpu.VMEM((2 * peers, 2 * count, chunk), BF16),
            pltpu.VMEM((count, 128), F32),
            pltpu.VMEM((peers, count, 128), F32),
            pltpu.VMEM((2, 2 * count, chunk), BF16),
            pltpu.VMEM((2 * peers, 2 * count, chunk), BF16),
            pltpu.VMEM((count, part), F32),
            pltpu.VMEM((count, part), F32),
            dma((9,)),
            dma((n, PIECES)),
            dma((peers, PIECES)),
            dma((n, PIECES)),
            dma((n, PIECES)),
            dma((2 * n, PIECES)),
            dma((2 * n, PIECES)),
        ]
        + [dma((peers,))] * 4
        + [dma((2 * peers,))] * 2
        + [dma((peers,))] * 2
        + [dma((2 * peers,))] * 2,
        compiler_params=pltpu.CompilerParams(
            collective_id=0, has_side_effects=True, vmem_limit_bytes=16 * 2**20
        ),
        cost_estimate=pl.CostEstimate(
            flops=2 * owned * width * (rank + count), bytes_accessed=6 * 2**20, transcendentals=0
        ),
    )(
        *[
            pltpu.with_memory_space_constraint(operand, pltpu.HBM)
            for operand in (
                lengths,
                hidden,
                query,
                incoming_key_value.reshape(rows, steps, both),
                cache.reshape(rows, span, both),
                output_projection_weight,
                adapter_down_factor,
                adapter_up_factor.T,
                gain.reshape(1, width),
            )
        ]
    )
    return pl.pallas_call(
        store_kernel,
        out_shape=(
            jax.ShapeDtypeStruct(normed.shape, BF16),
            jax.ShapeDtypeStruct(merged.shape, BF16),
        ),
        in_specs=[inside, inside],
        out_specs=(outside, outside),
        scratch_shapes=[dma((9,))],
        compiler_params=pltpu.CompilerParams(vmem_limit_bytes=16 * 2**20),
    )(normed, merged)


def solution(mesh):
    fits = mesh.shape["tensor"] == 4 and mesh.shape["replica"] == 4
    return jax.shard_map(
        fused if fits else per_device,
        mesh=mesh,
        in_specs=(
            P(("groups", "replica"), None, None),
            P(("groups", "replica"), None, "tensor"),
            P(("groups", "replica"), None, "tensor", None),
            P(("groups", "replica"), None, "tensor", None),
            P(("groups", "replica")),
            P("tensor", None),
            P(("groups", "tensor"), None),
            P(("groups", "tensor", "replica"), None),
            P(),
        ),
        out_specs=(P(("groups", "replica"), None, None), P(("groups", "tensor"), None)),
        check_vma=False,
    )
```
